32 devices in a mesh: grp: 2 (over x), ctx: 16 (over z, y, core).
Axes of the slice: x: 2, y: 2, z: 4, core: 2. Of those that a mesh axis runs over, the one named last changes fastest.
Arguments:
- seq_feats: bfloat16 [16384, 768], P(('grp', 'ctx')), may hold values from -6 to 6
- taps: float32 [7, 768], replicated, may hold values from -2 to 2
- pole_table: float32 [64], replicated, may hold values from 30 to 65536
- mode_index: int32 [256, 16], P(('grp', 'ctx')), may hold values from 0 to 63
- residues: float32 [256, 16], P(('grp', 'ctx')), may hold values from -1.5 to 1.5
- skip: float32 [256], P(('grp', 'ctx')), may hold values from 0.5 to 1.5
Outputs:
- mixer_out: bfloat16 [16384, 256], P(('grp', 'ctx'))
The draws below stay inside these ranges and needn't reach their ends.
All inputs are finite; a program needn't handle non-finite values.
Results may differ from the reference program's by a relative error of at most 0.005.
Values may be sent and summed in bfloat16 or wider, within the bound.
A program may use at most 128 MiB of HBM per device.

```python
import math
import jax
import jax.numpy as jnp
from jax import lax

TAPS = 7
MODES = 16
POLES = 64
SEQ = 16384
C = 256


def place_ends(result, stream_key, least, largest):
    place = [jax.random.randint(jax.random.fold_in(stream_key, axis), (), 0, length) for axis, length in enumerate(result.shape)]
    main_axis = result.shape.index(max(result.shape))
    neighbour = place[:main_axis] + [(place[main_axis] + 1) % result.shape[main_axis]] + place[main_axis + 1:]
    return result.at[tuple(place)].set(least).at[tuple(neighbour)].set(largest)


def block_levels(key, shape, shards, smallest, high):
    def one(position, parts):
        heights = jax.random.uniform(jax.random.fold_in(jax.random.fold_in(key, 6), position), (parts,), jnp.float32, smallest / len(shards), high / len(shards))
        return jnp.repeat(jnp.exp(heights), shape[position] // parts).reshape((-1,) + (1,) * (len(shape) - position - 1))

    factor_of = one(*shards[0])
    for cut in shards[1:]:
        factor_of = factor_of * one(*cut)
    return factor_of


def gaussian(key, extent, spread, limit, split=(), kind=jnp.bfloat16):
    entries = jax.random.normal(key, extent, jnp.float32) * spread
    if len(split) > 0:
        entries = block_levels(key, extent, split, -0.22, 0.18) * entries
    return jnp.clip(entries, min=-limit, max=limit).astype(kind)


def setup_inputs(seed: int = 0) -> dict:
    seeds = jax.random.split(jax.random.key(seed), 7)
    seq_feats = gaussian(seeds[0], (SEQ, 3 * C), 1.0, 6.0, ((0, 32),))
    taps = gaussian(seeds[1], (TAPS, 3 * C), TAPS ** -0.5, 2.0, (), jnp.float32)
    pole_table = jnp.clip(jnp.exp(jax.random.uniform(seeds[2], (POLES,), jnp.float32, math.log(30.0), math.log(65536.0))), 30.0, 65536.0)
    mode_index = place_ends(jax.random.randint(seeds[3], (C, MODES), 0, POLES), jax.random.fold_in(seeds[3], 1), 0, POLES - 1).astype(jnp.int32)
    residues = gaussian(seeds[4], (C, MODES), MODES ** -0.5, 1.5, ((0, 32),), jnp.float32)
    skip = jnp.clip(0.5 + 1.0 * jax.random.uniform(seeds[5], (C,), jnp.float32) ** block_levels(seeds[5], (C,), ((0, 32),), -0.2, 0.2), 0.5, 1.5)
    return dict(seq_feats=seq_feats, taps=taps, pole_table=pole_table, mode_index=mode_index, residues=residues, skip=skip)


def modal_filter(decay, residues, length):
    times = jnp.arange(length, dtype=jnp.float32)
    energy = jnp.expm1(-2.0 * length / decay) / jnp.expm1(-2.0 / decay)
    weights = residues / jnp.sqrt(energy)
    return lax.optimization_barrier(jnp.sum(weights[:, :, None] * jnp.exp(-times[None, None, :] / decay[:, :, None]), axis=1))

def reference(seq_feats, taps, pole_table, mode_index, residues, skip):
    seq, width3 = seq_feats.shape
    chans = width3 // 3
    ntaps = taps.shape[0]
    signal = seq_feats.astype(jnp.float32)
    padded = jnp.pad(signal, ((ntaps - 1, 0), (0, 0)))
    feats = jnp.zeros((seq, width3), jnp.float32)
    for shift_index in range(ntaps):
        start = ntaps - 1 - shift_index
        feats = feats + taps[shift_index][None, :] * padded[start:start + seq]
    query = feats[:, :chans]
    gated_low = (feats[:, chans:2 * chans] * feats[:, 2 * chans:]).astype(jnp.bfloat16)
    gated = lax.optimization_barrier(gated_low).astype(jnp.float32)
    decay = pole_table[mode_index]
    blocks = chans // 64
    gated_cols = gated.T.reshape(blocks, 64, seq)
    decay_blocks = decay.reshape(blocks, 64, -1)
    residue_blocks = residues.reshape(blocks, 64, -1)
    total = 2 * seq

    def one_block(items):
        signal_block, decay_block, residue_block = items
        filt = modal_filter(decay_block, residue_block, seq)
        spectrum = jnp.fft.rfft(signal_block, total) * jnp.fft.rfft(filt, total)
        return jnp.fft.irfft(spectrum, total)[:, :seq]
    conv = lax.map(one_block, (gated_cols, decay_blocks, residue_blocks)).reshape(chans, seq)
    mixed = conv + skip[:, None] * gated.T
    return (query * mixed.T).astype(jnp.bfloat16)
```

```python
import functools

import jax
import jax.numpy as jnp
from jax import lax
from jax.experimental import pallas as pl
from jax.experimental.pallas import tpu as pltpu
from jax.sharding import PartitionSpec as P

F32 = jnp.float32
BF16 = jnp.bfloat16
CHUNK = 32
ROWS = 64
COLS = 256
MESH = pl.DeviceIdType.MESH


def upper(value):
    return value.astype(BF16).astype(F32)


def paired(value, poles):
    high = upper(value)
    lane = lax.broadcasted_iota(jnp.int32, value.shape, 1)
    both = jnp.where(lane < poles, high, value - high).astype(BF16)
    return jnp.concatenate([both, both], axis=1)


def dot_last(left, right):
    return lax.dot_general(left, right, (((1,), (1,)), ((), ())), preferred_element_type=F32)


def kernel(
    outer, inner, x_ref, taps_ref, pole_ref, mode_ref, res_ref, skip_ref, out_ref,
    halo, wall, wsend, state, landed, turned, incoming,
    xs, gs, gb, grid, ys, qs, filt, acat, bcat, fcat, short,
    halo_send, halo_recv, w_send, w_recv, s_send, s_recv, x_send, x_recv,
):
    count = outer * inner
    tok, width3 = x_ref.shape
    chans = width3 // 3
    ntaps = taps_ref.shape[0]
    poles = pole_ref.shape[1]
    own, modes = mode_ref.shape
    seq = tok * count
    nchunk = tok // CHUNK
    me = lax.axis_index("grp") * inner + lax.axis_index("ctx")

    def where_is(index):
        return {"grp": index // inner, "ctx": lax.rem(index, inner)}

    barrier = pltpu.get_barrier_semaphore()

    def greet(step, carry):
        peer = lax.rem(me + step, count)
        pl.semaphore_signal(barrier, inc=1, device_id=where_is(peer), device_id_type=MESH)
        return carry

    lax.fori_loop(1, count, greet, 0)

    pole = jnp.concatenate([pole_ref[...], pole_ref[...]], axis=1)
    small = -2.0 / pole
    series = small * (1.0 + small * (0.5 + small * (1.0 / 6 + small * (1.0 / 24 + small * (
        1.0 / 120 + small * (1.0 / 720))))))
    energy = (jnp.exp(-2.0 * seq / pole) - 1.0) / series
    lane = lax.broadcasted_iota(jnp.int32, (own, 2 * poles), 1)
    entry = lax.rem(lane, poles)
    weight = jnp.zeros((own, 2 * poles), F32)
    for mode in range(modes):
        weight += jnp.where(mode_ref[:, mode : mode + 1] == entry, res_ref[:, mode : mode + 1], 0.0)
    weight = weight / jnp.sqrt(energy)
    diag = lax.broadcasted_iota(jnp.int32, (own, own), 0) == lax.broadcasted_iota(jnp.int32, (own, own), 1)
    skip_col = jnp.sum(jnp.where(diag, skip_ref[...], 0.0), axis=1, keepdims=True)
    mine = pl.ds(pl.multiple_of(me * own, own), own)
    wsend[...] = jnp.where(lane < poles, weight, jnp.where(lane == poles, skip_col, 0.0))
    wall[mine, :] = wsend[...]

    pl.semaphore_wait(barrier, count - 1)

    halo_copy = pltpu.make_async_remote_copy(
        src_ref=x_ref.at[tok - 16 :], dst_ref=halo, send_sem=halo_send, recv_sem=halo_recv,
        device_id=where_is(lax.rem(me + 1, count)), device_id_type=MESH,
    )

    @pl.when(me < count - 1)
    def _():
        halo_copy.start()

    @pl.when(me == 0)
    def _():
        halo[...] = jnp.zeros_like(halo)

    def push_weight(step, carry):
        peer = lax.rem(me + step, count)
        pltpu.make_async_remote_copy(
            src_ref=wsend, dst_ref=wall.at[mine, :], send_sem=w_send, recv_sem=w_recv,
            device_id=where_is(peer), device_id_type=MESH,
        ).start()
        return carry

    lax.fori_loop(1, count, push_weight, 0)

    square = lax.broadcasted_iota(jnp.int32, (poles, poles), 0) == lax.broadcasted_iota(
        jnp.int32, (poles, poles), 1)
    column = jnp.sum(jnp.where(square, pole_ref[...], 0.0), axis=1, keepdims=True)

    def ending(length):
        back = (length - 1 - lax.broadcasted_iota(jnp.int32, (poles, length), 1)).astype(F32)
        table = jnp.exp(-back / column)
        high = upper(table)
        return jnp.concatenate([high.astype(BF16), (table - high).astype(BF16)], axis=0)

    def starting(length, first):
        ahead = (first + lax.broadcasted_iota(jnp.int32, (length, 2 * poles), 0)).astype(F32)
        table = jnp.exp(-ahead / pole)
        high = upper(table)
        return jnp.concatenate([high.astype(BF16), (table - high).astype(BF16)], axis=1)

    acat[...] = ending(tok)
    short[...] = ending(CHUNK)
    bcat[...] = starting(tok, 1)
    fcat[...] = starting(CHUNK, 0)

    def fir(block, col):
        rows = xs[pl.ds(pl.multiple_of(block * ROWS, ROWS), ROWS + 8), col : col + COLS]
        total = jnp.zeros((ROWS, COLS), F32)
        for tap in range(ntaps):
            total += taps_ref[tap : tap + 1, col : col + COLS] * rows[8 - tap : 8 - tap + ROWS]
        return total

    def gate(block, carry):
        place = pl.ds(pl.multiple_of(block * ROWS, ROWS), ROWS)
        for col in range(0, chans, COLS):
            low = (fir(block, chans + col) * fir(block, 2 * chans + col)).astype(BF16)
            gb[place, col : col + COLS] = low
            wide = low.astype(F32)
            for part in range(0, COLS, 128):
                gs[(col + part) // 128, place, :] = wide[:, part : part + 128]
        return carry

    xs[8:, :] = x_ref[...].astype(F32)
    lax.fori_loop(1, tok // ROWS, gate, 0)

    @pl.when(me > 0)
    def _():
        halo_copy.wait_recv()

    xs[0:8, :] = halo[...].astype(F32)[8:16]
    gate(0, 0)

    state[...] = jnp.dot(acat[...], gb[...], preferred_element_type=F32).T
    landed[me] = state[mine, :]

    def push_state(step, carry):
        peer = lax.rem(me + step, count)
        pltpu.make_async_remote_copy(
            src_ref=state.at[pl.ds(pl.multiple_of(peer * own, own), own), :], dst_ref=landed.at[me],
            send_sem=s_send, recv_sem=s_recv,
            device_id=where_is(peer), device_id_type=MESH,
        ).start()
        return carry

    lax.fori_loop(1, count, push_state, 0)

    def query(block, carry):
        place = pl.ds(pl.multiple_of(block * ROWS, ROWS), ROWS)
        for col in range(0, chans, COLS):
            qs[place, col : col + COLS] = fir(block, col)
        return carry

    lax.fori_loop(0, tok // ROWS, query, 0)

    others = (count - 1) * own
    pltpu.make_async_copy(wall.at[0:others, :], wall.at[0:others, :], w_recv).wait()
    lane_all = lax.broadcasted_iota(jnp.int32, (chans, 2 * poles), 1)
    gathered = wall[...]
    twice = jnp.where(lane_all < poles, gathered, pltpu.roll(gathered, poles, 1))
    across = gathered.T
    by_pole = across[0:poles]
    first_row = lax.broadcasted_iota(jnp.int32, (CHUNK, chans), 0) == 0
    filt[...] = dot_last(fcat[...], paired(twice, poles)) + jnp.where(
        first_row, across[poles : poles + 1], 0.0)

    grid[0:CHUNK] = jnp.zeros((CHUNK, nchunk, chans), F32)
    for pos in range(CHUNK):
        for col in range(0, chans, 128):
            grid[CHUNK + pos, :, col : col + 128] = gs[col // 128, pl.ds(pos, nchunk, stride=CHUNK), :]

    def within(pos, carry):
        for col in range(0, chans, 128):
            total = jnp.zeros((nchunk, 128), F32)
            for lag in range(CHUNK):
                total += filt[lag : lag + 1, col : col + 128] * grid[CHUNK + pos - lag, :, col : col + 128]
            ys[col // 128, pl.ds(pos, nchunk, stride=CHUNK), :] = total
        return carry

    lax.fori_loop(0, CHUNK, within, 0)

    all_but_one = landed.at[0 : count - 1]
    pltpu.make_async_copy(all_but_one, all_but_one, s_recv).wait()
    jump = jnp.exp(-float(tok) / pole)
    running = jnp.zeros((own, 2 * poles), F32)
    for source in range(count):
        turned[source] = running * weight
        part = landed[source]
        running = running * jump + (part + pltpu.roll(part, poles, 1))
    incoming[mine, :] = turned[me]

    def push_turned(step, carry):
        peer = lax.rem(me + step, count)
        pltpu.make_async_remote_copy(
            src_ref=turned.at[peer], dst_ref=incoming.at[mine, :], send_sem=x_send, recv_sem=x_recv,
            device_id=where_is(peer), device_id_type=MESH,
        ).start()
        return carry

    lax.fori_loop(1, count, push_turned, 0)

    hop = jnp.exp(-float(CHUNK) / column)

    def between(chunk, carried):
        place = pl.ds(pl.multiple_of(chunk * CHUNK, CHUNK), CHUNK)
        high = carried.astype(BF16)
        low = (carried - high.astype(F32)).astype(BF16)
        stack = jnp.concatenate([high, low, high, low], axis=0)
        entering = jnp.dot(bcat[0:CHUNK, :], stack, preferred_element_type=F32)
        for col in range(0, chans, 128):
            ys[col // 128, place, :] += entering[:, col : col + 128]
        fresh = jnp.dot(short[...], gb[place, :], preferred_element_type=F32)
        return carried * hop + by_pole * (fresh[0:poles] + fresh[poles:])

    lax.fori_loop(0, nchunk, between, jnp.zeros((poles, chans), F32))

    pltpu.make_async_copy(incoming.at[0:others, :], incoming.at[0:others, :], x_recv).wait()
    stack = paired(incoming[...], poles)
    for row in range(0, tok, 128):
        conv = dot_last(bcat[row : row + 128, :], stack)
        for col in range(0, chans, 128):
            mixed = conv[:, col : col + 128] + ys[col // 128, row : row + 128, :]
            out_ref[row : row + 128, col : col + 128] = (
                qs[row : row + 128, col : col + 128] * mixed).astype(BF16)

    @pl.when(me < count - 1)
    def _():
        halo_copy.wait_send()

    pltpu.make_async_copy(wall.at[0:others, :], wall.at[0:others, :], w_send).wait()
    pltpu.make_async_copy(all_but_one, all_but_one, s_send).wait()
    pltpu.make_async_copy(incoming.at[0:others, :], incoming.at[0:others, :], x_send).wait()


def body(seq_feats, taps, pole_table, mode_index, residues, skip):
    tok, width3 = seq_feats.shape
    chans = width3 // 3
    outer = lax.axis_size("grp")
    inner = lax.axis_size("ctx")
    count = outer * inner
    poles = pole_table.shape[0]
    own = mode_index.shape[0]
    nchunk = tok // CHUNK
    vmem = pl.BlockSpec(memory_space=pltpu.VMEM)
    sem = pltpu.SemaphoreType.DMA
    return pl.pallas_call(
        functools.partial(kernel, outer, inner),
        out_shape=jax.ShapeDtypeStruct((tok, chans), BF16),
        in_specs=[vmem] * 6,
        out_specs=vmem,
        scratch_shapes=[
            pltpu.VMEM((16, width3), BF16),
            pltpu.VMEM((chans, 2 * poles), F32),
            pltpu.VMEM((own, 2 * poles), F32),
            pltpu.VMEM((chans, 2 * poles), F32),
            pltpu.VMEM((count, own, 2 * poles), F32),
            pltpu.VMEM((count, own, 2 * poles), F32),
            pltpu.VMEM((chans, 2 * poles), F32),
            pltpu.VMEM((tok + 8, width3), F32),
            pltpu.VMEM((chans // 128, tok, 128), F32),
            pltpu.VMEM((tok, chans), BF16),
            pltpu.VMEM((2 * CHUNK, nchunk, chans), F32),
            pltpu.VMEM((chans // 128, tok, 128), F32),
            pltpu.VMEM((tok, chans), F32),
            pltpu.VMEM((CHUNK, chans), F32),
            pltpu.VMEM((2 * poles, tok), BF16),
            pltpu.VMEM((tok, 4 * poles), BF16),
            pltpu.VMEM((CHUNK, 4 * poles), BF16),
            pltpu.VMEM((2 * poles, CHUNK), BF16),
        ] + [sem] * 8,
        compiler_params=pltpu.CompilerParams(
            collective_id=0, has_side_effects=True, vmem_limit_bytes=48 * 1024 * 1024
        ),
    )(
        seq_feats, taps, pole_table.reshape(1, poles), mode_index, residues, skip.reshape(1, own)
    )


def solution(mesh):
    return jax.shard_map(
        body,
        mesh=mesh,
        in_specs=(
            P(("grp", "ctx"), None),
            P(),
            P(),
            P(("grp", "ctx"), None),
            P(("grp", "ctx"), None),
            P(("grp", "ctx")),
        ),
        out_specs=P(("grp", "ctx"), None),
        check_vma=False,
    )
```

```python
import functools

import jax
import jax.numpy as jnp
from jax import lax
from jax.experimental import pallas as pl
from jax.experimental.pallas import tpu as pltpu
from jax.sharding import PartitionSpec as P

F32 = jnp.float32
BF16 = jnp.bfloat16
CHUNK = 32
ROWS = 64
GROUP = 8
COLS = 256
MESH = pl.DeviceIdType.MESH


def upper(value):
    return value.astype(BF16).astype(F32)


def paired(value, poles):
    high = upper(value)
    lane = lax.broadcasted_iota(jnp.int32, value.shape, 1)
    both = jnp.where(lane < poles, high, value - high).astype(BF16)
    return jnp.concatenate([both, both], axis=1)


def dot_last(left, right):
    return lax.dot_general(left, right, (((1,), (1,)), ((), ())), preferred_element_type=F32)


def kernel(
    outer, inner, x_hbm, taps_hbm, pole_hbm, mode_hbm, res_hbm, skip_hbm, out_ref,
    x_ref, taps_ref, pole_ref, mode_ref, res_ref, skip_ref, in_sems,
    halo, wall, wsend, state, landed, totals, turned, incoming,
    xs, gs, gb, grid, ys, qs, filt, acat, bcat, fcat, short,
    halo_send, halo_recv, w_send, w_recv, g_send, g_recv, s_send, s_recv, t_send, t_recv, x_send, x_recv,
):
    count = outer * inner
    operands = []
    for number, (source, target) in enumerate((
        (pole_hbm, pole_ref), (mode_hbm, mode_ref), (res_hbm, res_ref), (skip_hbm, skip_ref),
        (taps_hbm, taps_ref), (x_hbm, x_ref),
    )):
        operands.append(pltpu.make_async_copy(source, target, in_sems.at[number]))
        operands[-1].start()
    tok, width3 = x_ref.shape
    chans = width3 // 3
    ntaps = taps_ref.shape[0]
    poles = pole_ref.shape[1]
    own, modes = mode_ref.shape
    seq = tok * count
    nchunk = tok // CHUNK
    my_grp, my_ctx = lax.axis_index("grp"), lax.axis_index("ctx")
    me = my_grp * inner + my_ctx

    def wrapped(index, size):
        return jnp.where(index >= size, index - size, index)

    spans = inner // GROUP
    groups = outer * spans
    span, member = my_ctx // GROUP, lax.rem(my_ctx, GROUP)
    group = my_grp * spans + span
    share = chans // GROUP
    packed = share // 2

    def for_members(visit):
        for ahead in range(1, GROUP):
            peer = wrapped(member + ahead, GROUP)
            visit(peer, {"grp": my_grp, "ctx": span * GROUP + peer})

    def for_groups(visit):
        for ahead in range(outer):
            grp = wrapped(my_grp + ahead, outer)
            for further in range(1 if ahead == 0 else 0, spans):
                there = wrapped(span + further, spans)
                visit(grp * spans + there, {"grp": grp, "ctx": there * GROUP + member})

    def send(source, target, sent, received, place):
        pltpu.make_async_remote_copy(
            src_ref=source, dst_ref=target, send_sem=sent, recv_sem=received,
            device_id=place, device_id_type=MESH,
        ).start()

    def settle(ref, semaphore):
        pltpu.make_async_copy(ref, ref, semaphore).wait()

    behind = {
        "grp": jnp.where(my_ctx == 0, my_grp - 1, my_grp),
        "ctx": jnp.where(my_ctx == 0, inner - 1, my_ctx - 1),
    }
    barrier = pltpu.get_barrier_semaphore()

    def greet(peer, place):
        pl.semaphore_signal(barrier, inc=1, device_id=place, device_id_type=MESH)

    for_members(greet)
    for_groups(greet)

    @pl.when(me > 0)
    def _():
        greet(0, behind)

    for copy in operands[:4]:
        copy.wait()
    pole = jnp.concatenate([pole_ref[...], pole_ref[...]], axis=1)
    small = -2.0 / pole
    series = small * (1.0 + small * (0.5 + small * (1.0 / 6 + small * (1.0 / 24 + small * (
        1.0 / 120 + small * (1.0 / 720))))))
    energy = (jnp.exp(-2.0 * seq / pole) - 1.0) / series
    lane = lax.broadcasted_iota(jnp.int32, (own, 2 * poles), 1)
    entry = lax.rem(lane, poles)
    weight = jnp.zeros((own, 2 * poles), F32)
    for mode in range(modes):
        weight += jnp.where(mode_ref[:, mode : mode + 1] == entry, res_ref[:, mode : mode + 1], 0.0)
    weight = weight / jnp.sqrt(energy)
    diag = lax.broadcasted_iota(jnp.int32, (own, own), 0) == lax.broadcasted_iota(jnp.int32, (own, own), 1)
    skip_col = jnp.sum(jnp.where(diag, skip_ref[...], 0.0), axis=1, keepdims=True)
    wsend[...] = jnp.where(lane < poles, weight, jnp.where(lane == poles, skip_col, 0.0))
    wall[group, member] = wsend[...]

    grid[0:CHUNK] = jnp.zeros((CHUNK, nchunk, chans), F32)

    pl.semaphore_wait(barrier, GROUP - 1 + groups - 1 + jnp.where(me < count - 1, 1, 0))

    halo_copy = pltpu.make_async_remote_copy(
        src_ref=x_hbm.at[tok - 16 :], dst_ref=halo, send_sem=halo_send, recv_sem=halo_recv,
        device_id={
            "grp": wrapped(my_grp + jnp.where(my_ctx == inner - 1, 1, 0), outer),
            "ctx": wrapped(my_ctx + 1, inner),
        },
        device_id_type=MESH,
    )

    @pl.when(me < count - 1)
    def _():
        halo_copy.start()

    @pl.when(me == 0)
    def _():
        halo[...] = jnp.zeros_like(halo)

    def push_weight(peer, place):
        send(wsend, wall.at[group, member], w_send, w_recv, place)

    for_groups(push_weight)

    square = lax.broadcasted_iota(jnp.int32, (poles, poles), 0) == lax.broadcasted_iota(
        jnp.int32, (poles, poles), 1)
    column = jnp.sum(jnp.where(square, pole_ref[...], 0.0), axis=1, keepdims=True)

    def ending(length):
        back = (length - 1 - lax.broadcasted_iota(jnp.int32, (poles, length), 1)).astype(F32)
        table = jnp.exp(-back * (1.0 / column))
        high = upper(table)
        return jnp.concatenate([high.astype(BF16), (table - high).astype(BF16)], axis=0)

    def starting(length, first):
        ahead = (first + lax.broadcasted_iota(jnp.int32, (length, 2 * poles), 0)).astype(F32)
        table = jnp.exp(-ahead * (1.0 / pole))
        high = upper(table)
        return jnp.concatenate([high.astype(BF16), (table - high).astype(BF16)], axis=1)

    acat[...] = ending(tok)
    short[...] = ending(CHUNK)
    bcat[...] = starting(tok, 1)
    fcat[...] = starting(CHUNK, 0)

    def fir(block, col):
        rows = xs[pl.ds(pl.multiple_of(block * ROWS, ROWS), ROWS + 8), col : col + COLS]
        total = jnp.zeros((ROWS, COLS), F32)
        for tap in range(ntaps):
            total += taps_ref[tap : tap + 1, col : col + COLS] * rows[8 - tap : 8 - tap + ROWS]
        return total

    def gate(block, carry):
        place = pl.ds(pl.multiple_of(block * ROWS, ROWS), ROWS)
        for col in range(0, chans, COLS):
            low = (fir(block, chans + col) * fir(block, 2 * chans + col)).astype(BF16)
            gb[place, col : col + COLS] = low
            wide = low.astype(F32)
            for part in range(0, COLS, 128):
                gs[(col + part) // 128, place, :] = wide[:, part : part + 128]
        return carry

    for copy in operands[4:]:
        copy.wait()
    xs[8:, :] = x_ref[...].astype(F32)
    lax.fori_loop(1, tok // ROWS, gate, 0)

    @pl.when(me > 0)
    def _():
        halo_copy.wait_recv()

    xs[0:8, :] = halo[...].astype(F32)[8:16]
    gate(0, 0)

    ends = jnp.dot(acat[...], gb[...], preferred_element_type=F32).T
    ends = ends + pltpu.roll(ends, poles, 1)
    left_lanes = lax.broadcasted_iota(jnp.int32, (packed, 2 * poles), 1) < poles
    for index in range(GROUP):
        start = index * share
        state[index] = jnp.where(
            left_lanes, ends[start : start + packed], ends[start + packed : start + share])
    landed[member] = state[member]

    def push_state(peer, place):
        send(state.at[peer], landed.at[member], s_send, s_recv, place)

    for_members(push_state)

    settle(wall.at[0 : groups - 1, 0], w_recv)

    def push_gathered(peer, place):
        send(wall.at[:, member], wall.at[:, member], g_send, g_recv, place)

    for_members(push_gathered)

    def query(block, carry):
        place = pl.ds(pl.multiple_of(block * ROWS, ROWS), ROWS)
        for col in range(0, chans, COLS):
            qs[place, col : col + COLS] = fir(block, col)
        return carry

    lax.fori_loop(0, tok // ROWS, query, 0)

    for pos in range(CHUNK):
        for col in range(0, chans, 128):
            grid[CHUNK + pos, :, col : col + 128] = gs[col // 128, pl.ds(pos, nchunk, stride=CHUNK), :]

    settle(landed.at[0 : GROUP - 1], s_recv)
    jump = jnp.exp(-float(tok) / pole)
    total = landed[0]
    for source in range(1, GROUP):
        total = total * jump + landed[source]
    totals[group] = total

    def push_total(peer, place):
        send(totals.at[group], totals.at[group], t_send, t_recv, place)

    for_groups(push_total)

    settle(wall.at[:, 0 : GROUP - 1], g_recv)
    lane_all = lax.broadcasted_iota(jnp.int32, (chans, 2 * poles), 1)
    gathered = wall[...].reshape(chans, 2 * poles)
    twice = jnp.where(lane_all < poles, gathered, pltpu.roll(gathered, poles, 1))
    across = gathered.T
    by_pole = across[0:poles]
    first_row = lax.broadcasted_iota(jnp.int32, (CHUNK, chans), 0) == 0
    filt[...] = dot_last(fcat[...], paired(twice, poles)) + jnp.where(
        first_row, across[poles : poles + 1], 0.0)

    def within(pos, carry):
        for col in range(0, chans, 128):
            total = jnp.zeros((nchunk, 128), F32)
            for lag in range(CHUNK):
                total += filt[lag : lag + 1, col : col + 128] * grid[CHUNK + pos - lag, :, col : col + 128]
            ys[col // 128, pl.ds(pos, nchunk, stride=CHUNK), :] = total
        return carry

    lax.fori_loop(0, CHUNK, within, 0)

    settle(totals.at[0 : groups - 1], t_recv)
    leap = jnp.exp(-float(tok * GROUP) / pole)
    running = jnp.zeros((packed, 2 * poles), F32)
    for source in range(groups - 1):
        running = jnp.where(source < group, running * leap + totals[source], running)
    for source in range(GROUP):
        turned[source] = running
        running = running * jump + landed[source]
    incoming[member] = turned[member]

    def push_turned(peer, place):
        send(turned.at[peer], incoming.at[member], x_send, x_recv, place)

    for_members(push_turned)

    hop = jnp.exp(-float(CHUNK) / column)

    def between(chunk, carried):
        place = pl.ds(pl.multiple_of(chunk * CHUNK, CHUNK), CHUNK)
        high = carried.astype(BF16)
        low = (carried - high.astype(F32)).astype(BF16)
        stack = jnp.concatenate([high, low, high, low], axis=0)
        entering = jnp.dot(bcat[0:CHUNK, :], stack, preferred_element_type=F32)
        for col in range(0, chans, 128):
            ys[col // 128, place, :] += entering[:, col : col + 128]
        fresh = jnp.dot(short[...], gb[place, :], preferred_element_type=F32)
        return carried * hop + by_pole * (fresh[0:poles] + fresh[poles:])

    lax.fori_loop(0, nchunk, between, jnp.zeros((poles, chans), F32))

    settle(incoming.at[0 : GROUP - 1], x_recv)
    parts = []
    for index in range(GROUP):
        held = incoming[index]
        swapped = pltpu.roll(held, poles, 1)
        parts += [jnp.where(left_lanes, held, swapped), jnp.where(left_lanes, swapped, held)]
    stack = paired(jnp.concatenate(parts, axis=0) * twice, poles)
    for row in range(0, tok, 128):
        conv = dot_last(bcat[row : row + 128, :], stack)
        for col in range(0, chans, 128):
            mixed = conv[:, col : col + 128] + ys[col // 128, row : row + 128, :]
            out_ref[row : row + 128, col : col + 128] = (
                qs[row : row + 128, col : col + 128] * mixed).astype(BF16)

    @pl.when(me < count - 1)
    def _():
        halo_copy.wait_send()

    settle(wall.at[0 : groups - 1, 0], w_send)
    settle(wall.at[:, 0 : GROUP - 1], g_send)
    settle(landed.at[0 : GROUP - 1], s_send)
    settle(totals.at[0 : groups - 1], t_send)
    settle(incoming.at[0 : GROUP - 1], x_send)


def body(seq_feats, taps, pole_table, mode_index, residues, skip):
    tok, width3 = seq_feats.shape
    chans = width3 // 3
    outer = lax.axis_size("grp")
    inner = lax.axis_size("ctx")
    count = outer * inner
    poles = pole_table.shape[0]
    own = mode_index.shape[0]
    nchunk = tok // CHUNK
    groups, packed = count // GROUP, chans // GROUP // 2
    vmem = pl.BlockSpec(memory_space=pltpu.VMEM)
    sem = pltpu.SemaphoreType.DMA
    return pl.pallas_call(
        functools.partial(kernel, outer, inner),
        out_shape=jax.ShapeDtypeStruct((tok, chans), BF16),
        in_specs=[pl.BlockSpec(memory_space=pltpu.HBM)] * 6,
        out_specs=vmem,
        scratch_shapes=[
            pltpu.VMEM((tok, width3), BF16),
            pltpu.VMEM(taps.shape, F32),
            pltpu.VMEM((1, poles), F32),
            pltpu.VMEM(mode_index.shape, jnp.int32),
            pltpu.VMEM(residues.shape, F32),
            pltpu.VMEM((1, own), F32),
            sem((6,)),
            pltpu.VMEM((16, width3), BF16),
            pltpu.VMEM((groups, GROUP, own, 2 * poles), F32),
            pltpu.VMEM((own, 2 * poles), F32),
            pltpu.VMEM((GROUP, packed, 2 * poles), F32),
            pltpu.VMEM((GROUP, packed, 2 * poles), F32),
            pltpu.VMEM((groups, packed, 2 * poles), F32),
            pltpu.VMEM((GROUP, packed, 2 * poles), F32),
            pltpu.VMEM((GROUP, packed, 2 * poles), F32),
            pltpu.VMEM((tok + 8, width3), F32),
            pltpu.VMEM((chans // 128, tok, 128), F32),
            pltpu.VMEM((tok, chans), BF16),
            pltpu.VMEM((2 * CHUNK, nchunk, chans), F32),
            pltpu.VMEM((chans // 128, tok, 128), F32),
            pltpu.VMEM((tok, chans), F32),
            pltpu.VMEM((CHUNK, chans), F32),
            pltpu.VMEM((2 * poles, tok), BF16),
            pltpu.VMEM((tok, 4 * poles), BF16),
            pltpu.VMEM((CHUNK, 4 * poles), BF16),
            pltpu.VMEM((2 * poles, CHUNK), BF16),
        ] + [sem] * 12,
        compiler_params=pltpu.CompilerParams(
            collective_id=0, has_side_effects=True, vmem_limit_bytes=64 * 1024 * 1024
        ),
    )(
        seq_feats, taps, pole_table.reshape(1, poles), mode_index, residues, skip.reshape(1, own)
    )


def solution(mesh):
    return jax.shard_map(
        body,
        mesh=mesh,
        in_specs=(
            P(("grp", "ctx"), None),
            P(),
            P(),
            P(("grp", "ctx"), None),
            P(("grp", "ctx"), None),
            P(("grp", "ctx")),
        ),
        out_specs=P(("grp", "ctx"), None),
        check_vma=False,
    )
```

```python
import functools

import jax
import jax.numpy as jnp
from jax import lax
from jax.experimental import pallas as pl
from jax.experimental.pallas import tpu as pltpu
from jax.sharding import PartitionSpec as P

F32 = jnp.float32
BF16 = jnp.bfloat16
CHUNK = 32
ROWS = 64
GROUP = 8
COLS = 256
MESH = pl.DeviceIdType.MESH


def upper(value):
    return value.astype(BF16).astype(F32)


def paired(value, poles):
    high = upper(value)
    lane = lax.broadcasted_iota(jnp.int32, value.shape, 1)
    both = jnp.where(lane < poles, high, value - high).astype(BF16)
    return jnp.concatenate([both, both], axis=1)


def dot_last(left, right):
    return lax.dot_general(left, right, (((1,), (1,)), ((), ())), preferred_element_type=F32)


def kernel(
    outer, inner, x_hbm, taps_hbm, pole_hbm, mode_hbm, res_hbm, skip_hbm, out_hbm, out_ref, out_sems,
    x_ref, taps_ref, pole_ref, mode_ref, res_ref, skip_ref, in_sems,
    halo, wall, wsend, state, landed, totals, turned, incoming,
    xs, gs, gb, grid, ys, qs, filt, acat, bcat, fcat, short,
    halo_send, halo_recv, w_send, w_recv, g_send, g_recv, s_send, s_recv, t_send, t_recv, x_send, x_recv,
):
    count = outer * inner
    operands = []
    for number, (source, target) in enumerate((
        (pole_hbm, pole_ref), (mode_hbm, mode_ref), (res_hbm, res_ref), (skip_hbm, skip_ref),
        (taps_hbm, taps_ref), (x_hbm, x_ref),
    )):
        operands.append(pltpu.make_async_copy(source, target, in_sems.at[number]))
        operands[-1].start()
    tok, width3 = x_ref.shape
    chans = width3 // 3
    ntaps = taps_ref.shape[0]
    poles = pole_ref.shape[1]
    own, modes = mode_ref.shape
    seq = tok * count
    nchunk = tok // CHUNK
    my_grp, my_ctx = lax.axis_index("grp"), lax.axis_index("ctx")
    me = my_grp * inner + my_ctx

    def wrapped(index, size):
        return jnp.where(index >= size, index - size, index)

    spans = inner // GROUP
    groups = outer * spans
    span, member = my_ctx // GROUP, lax.rem(my_ctx, GROUP)
    group = my_grp * spans + span
    share = chans // GROUP
    packed = share // 2

    def for_members(visit):
        for ahead in range(1, GROUP):
            peer = wrapped(member + ahead, GROUP)
            visit(peer, {"grp": my_grp, "ctx": span * GROUP + peer})

    def for_groups(visit):
        for ahead in range(outer):
            grp = wrapped(my_grp + ahead, outer)
            for further in range(1 if ahead == 0 else 0, spans):
                there = wrapped(span + further, spans)
                visit(grp * spans + there, {"grp": grp, "ctx": there * GROUP + member})

    def send(source, target, sent, received, place):
        pltpu.make_async_remote_copy(
            src_ref=source, dst_ref=target, send_sem=sent, recv_sem=received,
            device_id=place, device_id_type=MESH,
        ).start()

    def settle(ref, semaphore):
        pltpu.make_async_copy(ref, ref, semaphore).wait()

    behind = {
        "grp": jnp.where(my_ctx == 0, my_grp - 1, my_grp),
        "ctx": jnp.where(my_ctx == 0, inner - 1, my_ctx - 1),
    }
    barrier = pltpu.get_barrier_semaphore()

    def greet(peer, place):
        pl.semaphore_signal(barrier, inc=1, device_id=place, device_id_type=MESH)

    for_members(greet)
    for_groups(greet)

    @pl.when(me > 0)
    def _():
        greet(0, behind)

    for copy in operands[:4]:
        copy.wait()
    pole = jnp.concatenate([pole_ref[...], pole_ref[...]], axis=1)
    small = -2.0 / pole
    series = small * (1.0 + small * (0.5 + small * (1.0 / 6 + small * (1.0 / 24 + small * (
        1.0 / 120 + small * (1.0 / 720))))))
    energy = (jnp.exp(-2.0 * seq / pole) - 1.0) / series
    lane = lax.broadcasted_iota(jnp.int32, (own, 2 * poles), 1)
    entry = lax.rem(lane, poles)
    weight = jnp.zeros((own, 2 * poles), F32)
    for mode in range(modes):
        weight += jnp.where(mode_ref[:, mode : mode + 1] == entry, res_ref[:, mode : mode + 1], 0.0)
    weight = weight / jnp.sqrt(energy)
    diag = lax.broadcasted_iota(jnp.int32, (own, own), 0) == lax.broadcasted_iota(jnp.int32, (own, own), 1)
    skip_col = jnp.sum(jnp.where(diag, skip_ref[...], 0.0), axis=1, keepdims=True)
    wsend[...] = jnp.where(lane < poles, weight, jnp.where(lane == poles, skip_col, 0.0))
    wall[group, member] = wsend[...]


    square = lax.broadcasted_iota(jnp.int32, (poles, poles), 0) == lax.broadcasted_iota(
        jnp.int32, (poles, poles), 1)
    column = jnp.sum(jnp.where(square, pole_ref[...], 0.0), axis=1, keepdims=True)

    def ending(length):
        back = (length - 1 - lax.broadcasted_iota(jnp.int32, (poles, length), 1)).astype(F32)
        table = jnp.exp(-back * (1.0 / column))
        high = upper(table)
        return jnp.concatenate([high.astype(BF16), (table - high).astype(BF16)], axis=0)

    def starting(length, first):
        ahead = (first + lax.broadcasted_iota(jnp.int32, (length, 2 * poles), 0)).astype(F32)
        table = jnp.exp(-ahead * (1.0 / pole))
        high = upper(table)
        return jnp.concatenate([high.astype(BF16), (table - high).astype(BF16)], axis=1)

    acat[...] = ending(tok)

    for copy in operands[4:]:
        copy.wait()
    xs[8:, chans:] = x_ref[:, chans:].astype(F32)

    pl.semaphore_wait(barrier, GROUP - 1 + groups - 1 + jnp.where(me < count - 1, 1, 0))

    halo_copy = pltpu.make_async_remote_copy(
        src_ref=x_hbm.at[tok - 16 :], dst_ref=halo, send_sem=halo_send, recv_sem=halo_recv,
        device_id={
            "grp": wrapped(my_grp + jnp.where(my_ctx == inner - 1, 1, 0), outer),
            "ctx": wrapped(my_ctx + 1, inner),
        },
        device_id_type=MESH,
    )

    @pl.when(me < count - 1)
    def _():
        halo_copy.start()

    @pl.when(me == 0)
    def _():
        halo[...] = jnp.zeros_like(halo)

    def push_weight(peer, place):
        send(wsend, wall.at[group, member], w_send, w_recv, place)

    for_groups(push_weight)

    def fir(block, col):
        rows = xs[pl.ds(pl.multiple_of(block * ROWS, ROWS), ROWS + 8), col : col + COLS]
        total = jnp.zeros((ROWS, COLS), F32)
        for tap in range(ntaps):
            total += taps_ref[tap : tap + 1, col : col + COLS] * rows[8 - tap : 8 - tap + ROWS]
        return total

    def gate(block, carry):
        place = pl.ds(pl.multiple_of(block * ROWS, ROWS), ROWS)
        for col in range(0, chans, COLS):
            low = (fir(block, chans + col) * fir(block, 2 * chans + col)).astype(BF16)
            gb[place, col : col + COLS] = low
            wide = low.astype(F32)
            for part in range(0, COLS, 128):
                gs[(col + part) // 128, place, :] = wide[:, part : part + 128]
        return carry

    lax.fori_loop(1, tok // ROWS, gate, 0)

    @pl.when(me > 0)
    def _():
        halo_copy.wait_recv()

    xs[0:8, :] = halo[...].astype(F32)[8:16]
    gate(0, 0)

    ends = jnp.dot(acat[...], gb[...], preferred_element_type=F32).T
    ends = ends + pltpu.roll(ends, poles, 1)
    left_lanes = lax.broadcasted_iota(jnp.int32, (packed, 2 * poles), 1) < poles
    for index in range(GROUP):
        start = index * share
        state[index] = jnp.where(
            left_lanes, ends[start : start + packed], ends[start + packed : start + share])
    landed[member] = state[member]

    def push_state(peer, place):
        send(state.at[peer], landed.at[member], s_send, s_recv, place)

    for_members(push_state)

    settle(wall.at[0 : groups - 1, 0], w_recv)

    def push_gathered(peer, place):
        send(wall.at[:, member], wall.at[:, member], g_send, g_recv, place)

    for_members(push_gathered)

    short[...] = ending(CHUNK)
    bcat[...] = starting(tok, 1)
    fcat[...] = starting(CHUNK, 0)
    grid[0:CHUNK] = jnp.zeros((CHUNK, nchunk, chans), F32)
    xs[8:, 0:chans] = x_ref[:, 0:chans].astype(F32)

    def query(block, carry):
        place = pl.ds(pl.multiple_of(block * ROWS, ROWS), ROWS)
        for col in range(0, chans, COLS):
            qs[place, col : col + COLS] = fir(block, col)
        return carry

    lax.fori_loop(0, tok // ROWS, query, 0)

    for pos in range(CHUNK):
        for col in range(0, chans, 128):
            grid[CHUNK + pos, :, col : col + 128] = gs[col // 128, pl.ds(pos, nchunk, stride=CHUNK), :]

    settle(landed.at[0 : GROUP - 1], s_recv)
    jump = jnp.exp(-float(tok) / pole)
    total = landed[0]
    for source in range(1, GROUP):
        total = total * jump + landed[source]
    totals[group] = total

    def push_total(peer, place):
        send(totals.at[group], totals.at[group], t_send, t_recv, place)

    for_groups(push_total)

    settle(wall.at[:, 0 : GROUP - 1], g_recv)
    lane_all = lax.broadcasted_iota(jnp.int32, (chans, 2 * poles), 1)
    gathered = wall[...].reshape(chans, 2 * poles)
    twice = jnp.where(lane_all < poles, gathered, pltpu.roll(gathered, poles, 1))
    across = gathered.T
    by_pole = across[0:poles]
    first_row = lax.broadcasted_iota(jnp.int32, (CHUNK, chans), 0) == 0
    filt[...] = dot_last(fcat[...], paired(twice, poles)) + jnp.where(
        first_row, across[poles : poles + 1], 0.0)

    def within(pos, carry):
        for col in range(0, chans, 128):
            total = jnp.zeros((nchunk, 128), F32)
            for lag in range(CHUNK):
                total += filt[lag : lag + 1, col : col + 128] * grid[CHUNK + pos - lag, :, col : col + 128]
            ys[col // 128, pl.ds(pos, nchunk, stride=CHUNK), :] = total
        return carry

    lax.fori_loop(0, CHUNK, within, 0)

    settle(totals.at[0 : groups - 1], t_recv)
    leap = jnp.exp(-float(tok * GROUP) / pole)
    running = jnp.zeros((packed, 2 * poles), F32)
    for source in range(groups - 1):
        running = jnp.where(source < group, running * leap + totals[source], running)
    for source in range(GROUP):
        turned[source] = running
        running = running * jump + landed[source]
    incoming[member] = turned[member]

    def push_turned(peer, place):
        send(turned.at[peer], incoming.at[member], x_send, x_recv, place)

    for_members(push_turned)

    hop = jnp.exp(-float(CHUNK) / column)

    def between(chunk, carried):
        place = pl.ds(pl.multiple_of(chunk * CHUNK, CHUNK), CHUNK)
        high = carried.astype(BF16)
        low = (carried - high.astype(F32)).astype(BF16)
        stack = jnp.concatenate([high, low, high, low], axis=0)
        entering = jnp.dot(bcat[0:CHUNK, :], stack, preferred_element_type=F32)
        for col in range(0, chans, 128):
            ys[col // 128, place, :] += entering[:, col : col + 128]
        fresh = jnp.dot(short[...], gb[place, :], preferred_element_type=F32)
        return carried * hop + by_pole * (fresh[0:poles] + fresh[poles:])

    lax.fori_loop(0, nchunk, between, jnp.zeros((poles, chans), F32))

    settle(incoming.at[0 : GROUP - 1], x_recv)
    parts = []
    for index in range(GROUP):
        held = incoming[index]
        swapped = pltpu.roll(held, poles, 1)
        parts += [jnp.where(left_lanes, held, swapped), jnp.where(left_lanes, swapped, held)]
    stack = paired(jnp.concatenate(parts, axis=0) * twice, poles)
    results = []
    for row in range(0, tok, 128):
        conv = dot_last(bcat[row : row + 128, :], stack)
        for col in range(0, chans, 128):
            mixed = conv[:, col : col + 128] + ys[col // 128, row : row + 128, :]
            out_ref[row : row + 128, col : col + 128] = (
                qs[row : row + 128, col : col + 128] * mixed).astype(BF16)
        results.append(pltpu.make_async_copy(
            out_ref.at[row : row + 128], out_hbm.at[row : row + 128], out_sems.at[row // 128]))
        results[-1].start()

    @pl.when(me < count - 1)
    def _():
        halo_copy.wait_send()

    settle(wall.at[0 : groups - 1, 0], w_send)
    settle(wall.at[:, 0 : GROUP - 1], g_send)
    settle(landed.at[0 : GROUP - 1], s_send)
    settle(totals.at[0 : groups - 1], t_send)
    settle(incoming.at[0 : GROUP - 1], x_send)
    for copy in results:
        copy.wait()


def body(seq_feats, taps, pole_table, mode_index, residues, skip):
    tok, width3 = seq_feats.shape
    chans = width3 // 3
    outer = lax.axis_size("grp")
    inner = lax.axis_size("ctx")
    count = outer * inner
    poles = pole_table.shape[0]
    own = mode_index.shape[0]
    nchunk = tok // CHUNK
    groups, packed = count // GROUP, chans // GROUP // 2
    sem = pltpu.SemaphoreType.DMA
    return pl.pallas_call(
        functools.partial(kernel, outer, inner),
        out_shape=jax.ShapeDtypeStruct((tok, chans), BF16),
        in_specs=[pl.BlockSpec(memory_space=pltpu.HBM)] * 6,
        out_specs=pl.BlockSpec(memory_space=pltpu.HBM),
        scratch_shapes=[
            pltpu.VMEM((tok, chans), BF16),
            sem((tok // 128,)),
            pltpu.VMEM((tok, width3), BF16),
            pltpu.VMEM(taps.shape, F32),
            pltpu.VMEM((1, poles), F32),
            pltpu.VMEM(mode_index.shape, jnp.int32),
            pltpu.VMEM(residues.shape, F32),
            pltpu.VMEM((1, own), F32),
            sem((6,)),
            pltpu.VMEM((16, width3), BF16),
            pltpu.VMEM((groups, GROUP, own, 2 * poles), F32),
            pltpu.VMEM((own, 2 * poles), F32),
            pltpu.VMEM((GROUP, packed, 2 * poles), F32),
            pltpu.VMEM((GROUP, packed, 2 * poles), F32),
            pltpu.VMEM((groups, packed, 2 * poles), F32),
            pltpu.VMEM((GROUP, packed, 2 * poles), F32),
            pltpu.VMEM((GROUP, packed, 2 * poles), F32),
            pltpu.VMEM((tok + 8, width3), F32),
            pltpu.VMEM((chans // 128, tok, 128), F32),
            pltpu.VMEM((tok, chans), BF16),
            pltpu.VMEM((2 * CHUNK, nchunk, chans), F32),
            pltpu.VMEM((chans // 128, tok, 128), F32),
            pltpu.VMEM((tok, chans), F32),
            pltpu.VMEM((CHUNK, chans), F32),
            pltpu.VMEM((2 * poles, tok), BF16),
            pltpu.VMEM((tok, 4 * poles), BF16),
            pltpu.VMEM((CHUNK, 4 * poles), BF16),
            pltpu.VMEM((2 * poles, CHUNK), BF16),
        ] + [sem] * 12,
        compiler_params=pltpu.CompilerParams(
            collective_id=0, has_side_effects=True, vmem_limit_bytes=64 * 1024 * 1024
        ),
    )(
        seq_feats, taps, pole_table.reshape(1, poles), mode_index, residues, skip.reshape(1, own)
    )


def solution(mesh):
    return jax.shard_map(
        body,
        mesh=mesh,
        in_specs=(
            P(("grp", "ctx"), None),
            P(),
            P(),
            P(("grp", "ctx"), None),
            P(("grp", "ctx"), None),
            P(("grp", "ctx")),
        ),
        out_specs=P(("grp", "ctx"), None),
        check_vma=False,
    )
```

```python
import functools

import jax
import jax.numpy as jnp
from jax import lax
from jax.experimental import pallas as pl
from jax.experimental.pallas import tpu as pltpu
from jax.sharding import PartitionSpec as P

F32 = jnp.float32
BF16 = jnp.bfloat16
CHUNK = 32
ROWS = 64
GROUP = 8
COLS = 256
MESH = pl.DeviceIdType.MESH


def upper(value):
    return value.astype(BF16).astype(F32)


def paired(value, poles):
    high = upper(value)
    lane = lax.broadcasted_iota(jnp.int32, value.shape, 1)
    both = jnp.where(lane < poles, high, value - high).astype(BF16)
    return jnp.concatenate([both, both], axis=1)


def dot_last(left, right):
    return lax.dot_general(left, right, (((1,), (1,)), ((), ())), preferred_element_type=F32)


def kernel(
    outer, inner, x_hbm, taps_hbm, pole_hbm, mode_hbm, res_hbm, skip_hbm, out_hbm, out_ref, out_sems,
    x_ref, taps_ref, pole_ref, mode_ref, res_ref, skip_ref, in_sems,
    halo, wall, wsend, state, landed, totals, turned, incoming,
    xs, gs, gb, grid, ys, qs, filt, acat, bcat, fcat, short,
    halo_send, halo_recv, w_send, w_recv, g_send, g_recv, s_send, s_recv, t_send, t_recv, x_send, x_recv,
):
    count = outer * inner
    tok, width3 = x_ref.shape
    chans = width3 // 3
    ntaps = taps_ref.shape[0]
    poles = pole_ref.shape[1]
    own, modes = mode_ref.shape
    seq = tok * count
    nchunk = tok // CHUNK
    my_grp, my_ctx = lax.axis_index("grp"), lax.axis_index("ctx")
    me = my_grp * inner + my_ctx

    def wrapped(index, size):
        return jnp.where(index >= size, index - size, index)

    spans = inner // GROUP
    groups = outer * spans
    span, member = my_ctx // GROUP, lax.rem(my_ctx, GROUP)
    group = my_grp * spans + span
    share = chans // GROUP
    packed = share // 2

    def for_members(visit):
        for ahead in range(1, GROUP):
            peer = wrapped(member + ahead, GROUP)
            visit(peer, {"grp": my_grp, "ctx": span * GROUP + peer})

    def for_groups(visit):
        for ahead in range(outer):
            grp = wrapped(my_grp + ahead, outer)
            for further in range(1 if ahead == 0 else 0, spans):
                there = wrapped(span + further, spans)
                visit(grp * spans + there, {"grp": grp, "ctx": there * GROUP + member})

    def send(source, target, sent, received, place):
        pltpu.make_async_remote_copy(
            src_ref=source, dst_ref=target, send_sem=sent, recv_sem=received,
            device_id=place, device_id_type=MESH,
        ).start()

    def settle(ref, semaphore):
        pltpu.make_async_copy(ref, ref, semaphore).wait()

    behind = {
        "grp": jnp.where(my_ctx == 0, my_grp - 1, my_grp),
        "ctx": jnp.where(my_ctx == 0, inner - 1, my_ctx - 1),
    }
    barrier = pltpu.get_barrier_semaphore()

    def greet(peer, place):
        pl.semaphore_signal(barrier, inc=1, device_id=place, device_id_type=MESH)

    for_groups(greet)
    for_members(greet)

    @pl.when(me > 0)
    def _():
        greet(0, behind)

    operands = []
    for number, (source, target) in enumerate((
        (pole_hbm, pole_ref), (mode_hbm, mode_ref), (res_hbm, res_ref), (skip_hbm, skip_ref),
        (taps_hbm, taps_ref), (x_hbm, x_ref),
    )):
        operands.append(pltpu.make_async_copy(source, target, in_sems.at[number]))
        operands[-1].start()
    for copy in operands[:4]:
        copy.wait()
    pole = jnp.concatenate([pole_ref[...], pole_ref[...]], axis=1)
    small = -2.0 / pole
    series = small * (1.0 + small * (0.5 + small * (1.0 / 6 + small * (1.0 / 24 + small * (
        1.0 / 120 + small * (1.0 / 720))))))
    energy = (jnp.exp(-2.0 * seq / pole) - 1.0) / series
    lane = lax.broadcasted_iota(jnp.int32, (own, 2 * poles), 1)
    entry = lax.rem(lane, poles)
    weight = jnp.zeros((own, 2 * poles), F32)
    for mode in range(modes):
        weight += jnp.where(mode_ref[:, mode : mode + 1] == entry, res_ref[:, mode : mode + 1], 0.0)
    weight = weight / jnp.sqrt(energy)
    diag = lax.broadcasted_iota(jnp.int32, (own, own), 0) == lax.broadcasted_iota(jnp.int32, (own, own), 1)
    skip_col = jnp.sum(jnp.where(diag, skip_ref[...], 0.0), axis=1, keepdims=True)
    wsend[...] = jnp.where(lane < poles, weight, jnp.where(lane == poles, skip_col, 0.0))
    wall[group, member] = wsend[...]


    square = lax.broadcasted_iota(jnp.int32, (poles, poles), 0) == lax.broadcasted_iota(
        jnp.int32, (poles, poles), 1)
    column = jnp.sum(jnp.where(square, pole_ref[...], 0.0), axis=1, keepdims=True)

    def ending(length):
        back = (length - 1 - lax.broadcasted_iota(jnp.int32, (poles, length), 1)).astype(F32)
        table = jnp.exp(-back * (1.0 / column))
        high = upper(table)
        return jnp.concatenate([high.astype(BF16), (table - high).astype(BF16)], axis=0)

    def starting(length, first):
        ahead = (first + lax.broadcasted_iota(jnp.int32, (length, 2 * poles), 0)).astype(F32)
        table = jnp.exp(-ahead * (1.0 / pole))
        high = upper(table)
        return jnp.concatenate([high.astype(BF16), (table - high).astype(BF16)], axis=1)

    acat[...] = ending(tok)

    for copy in operands[4:]:
        copy.wait()
    xs[8:, chans:] = x_ref[:, chans:].astype(F32)

    pl.semaphore_wait(barrier, GROUP - 1 + groups - 1 + jnp.where(me < count - 1, 1, 0))

    halo_copy = pltpu.make_async_remote_copy(
        src_ref=x_hbm.at[tok - 16 :], dst_ref=halo, send_sem=halo_send, recv_sem=halo_recv,
        device_id={
            "grp": wrapped(my_grp + jnp.where(my_ctx == inner - 1, 1, 0), outer),
            "ctx": wrapped(my_ctx + 1, inner),
        },
        device_id_type=MESH,
    )

    @pl.when(me < count - 1)
    def _():
        halo_copy.start()

    @pl.when(me == 0)
    def _():
        halo[...] = jnp.zeros_like(halo)

    def push_weight(peer, place):
        send(wsend, wall.at[group, member], w_send, w_recv, place)

    for_groups(push_weight)

    def fir(block, col):
        rows = xs[pl.ds(pl.multiple_of(block * ROWS, ROWS), ROWS + 8), col : col + COLS]
        total = jnp.zeros((ROWS, COLS), F32)
        for tap in range(ntaps):
            total += taps_ref[tap : tap + 1, col : col + COLS] * rows[8 - tap : 8 - tap + ROWS]
        return total

    def gate(block, carry):
        place = pl.ds(pl.multiple_of(block * ROWS, ROWS), ROWS)
        for col in range(0, chans, COLS):
            low = (fir(block, chans + col) * fir(block, 2 * chans + col)).astype(BF16)
            gb[place, col : col + COLS] = low
            wide = low.astype(F32)
            for part in range(0, COLS, 128):
                gs[(col + part) // 128, place, :] = wide[:, part : part + 128]
        return carry

    lax.fori_loop(1, tok // ROWS, gate, 0)

    @pl.when(me > 0)
    def _():
        halo_copy.wait_recv()

    xs[0:8, :] = halo[...].astype(F32)[8:16]
    gate(0, 0)

    ends = jnp.dot(acat[...], gb[...], preferred_element_type=F32).T
    ends = ends + pltpu.roll(ends, poles, 1)
    left_lanes = lax.broadcasted_iota(jnp.int32, (packed, 2 * poles), 1) < poles
    for index in range(GROUP):
        start = index * share
        state[index] = jnp.where(
            left_lanes, ends[start : start + packed], ends[start + packed : start + share])
    landed[member] = state[member]

    def push_state(peer, place):
        send(state.at[peer], landed.at[member], s_send, s_recv, place)

    for_members(push_state)

    settle(wall.at[0 : groups - 1, 0], w_recv)

    def push_gathered(peer, place):
        send(wall.at[:, member], wall.at[:, member], g_send, g_recv, place)

    for_members(push_gathered)

    short[...] = ending(CHUNK)
    bcat[...] = starting(tok, 1)
    fcat[...] = starting(CHUNK, 0)
    grid[0:CHUNK] = jnp.zeros((CHUNK, nchunk, chans), F32)
    xs[8:, 0:chans] = x_ref[:, 0:chans].astype(F32)

    def query(block, carry):
        place = pl.ds(pl.multiple_of(block * ROWS, ROWS), ROWS)
        for col in range(0, chans, COLS):
            qs[place, col : col + COLS] = fir(block, col)
        return carry

    lax.fori_loop(0, tok // ROWS, query, 0)

    for pos in range(CHUNK):
        for col in range(0, chans, 128):
            grid[CHUNK + pos, :, col : col + 128] = gs[col // 128, pl.ds(pos, nchunk, stride=CHUNK), :]

    settle(landed.at[0 : GROUP - 1], s_recv)
    jump = jnp.exp(-float(tok) / pole)
    total = landed[0]
    for source in range(1, GROUP):
        total = total * jump + landed[source]
    totals[group] = total

    def push_total(peer, place):
        send(totals.at[group], totals.at[group], t_send, t_recv, place)

    for_groups(push_total)

    settle(wall.at[:, 0 : GROUP - 1], g_recv)
    lane_all = lax.broadcasted_iota(jnp.int32, (chans, 2 * poles), 1)
    gathered = wall[...].reshape(chans, 2 * poles)
    twice = jnp.where(lane_all < poles, gathered, pltpu.roll(gathered, poles, 1))
    across = gathered.T
    by_pole = across[0:poles]
    first_row = lax.broadcasted_iota(jnp.int32, (CHUNK, chans), 0) == 0
    filt[...] = dot_last(fcat[...], paired(twice, poles)) + jnp.where(
        first_row, across[poles : poles + 1], 0.0)

    def within(pos, carry):
        for col in range(0, chans, 128):
            total = jnp.zeros((nchunk, 128), F32)
            for lag in range(CHUNK):
                total += filt[lag : lag + 1, col : col + 128] * grid[CHUNK + pos - lag, :, col : col + 128]
            ys[col // 128, pl.ds(pos, nchunk, stride=CHUNK), :] = total
        return carry

    lax.fori_loop(0, CHUNK, within, 0)

    settle(totals.at[0 : groups - 1], t_recv)
    leap = jnp.exp(-float(tok * GROUP) / pole)
    running = jnp.zeros((packed, 2 * poles), F32)
    for source in range(groups - 1):
        running = jnp.where(source < group, running * leap + totals[source], running)
    for source in range(GROUP):
        turned[source] = running
        running = running * jump + landed[source]
    incoming[member] = turned[member]

    def push_turned(peer, place):
        send(turned.at[peer], incoming.at[member], x_send, x_recv, place)

    for_members(push_turned)

    hop = jnp.exp(-float(CHUNK) / column)

    def between(chunk, carried):
        place = pl.ds(pl.multiple_of(chunk * CHUNK, CHUNK), CHUNK)
        high = carried.astype(BF16)
        low = (carried - high.astype(F32)).astype(BF16)
        stack = jnp.concatenate([high, low, high, low], axis=0)
        entering = jnp.dot(bcat[0:CHUNK, :], stack, preferred_element_type=F32)
        for col in range(0, chans, 128):
            ys[col // 128, place, :] += entering[:, col : col + 128]
        fresh = jnp.dot(short[...], gb[place, :], preferred_element_type=F32)
        return carried * hop + by_pole * (fresh[0:poles] + fresh[poles:])

    lax.fori_loop(0, nchunk, between, jnp.zeros((poles, chans), F32))

    settle(incoming.at[0 : GROUP - 1], x_recv)
    parts = []
    for index in range(GROUP):
        held = incoming[index]
        swapped = pltpu.roll(held, poles, 1)
        parts += [jnp.where(left_lanes, held, swapped), jnp.where(left_lanes, swapped, held)]
    stack = paired(jnp.concatenate(parts, axis=0) * twice, poles)
    results = []
    for row in range(0, tok, 128):
        conv = dot_last(bcat[row : row + 128, :], stack)
        for col in range(0, chans, 128):
            mixed = conv[:, col : col + 128] + ys[col // 128, row : row + 128, :]
            out_ref[row : row + 128, col : col + 128] = (
                qs[row : row + 128, col : col + 128] * mixed).astype(BF16)
        results.append(pltpu.make_async_copy(
            out_ref.at[row : row + 128], out_hbm.at[row : row + 128], out_sems.at[row // 128]))
        results[-1].start()

    @pl.when(me < count - 1)
    def _():
        halo_copy.wait_send()

    settle(wall.at[0 : groups - 1, 0], w_send)
    settle(wall.at[:, 0 : GROUP - 1], g_send)
    settle(landed.at[0 : GROUP - 1], s_send)
    settle(totals.at[0 : groups - 1], t_send)
    settle(incoming.at[0 : GROUP - 1], x_send)
    for copy in results:
        copy.wait()


def body(seq_feats, taps, pole_table, mode_index, residues, skip):
    tok, width3 = seq_feats.shape
    chans = width3 // 3
    outer = lax.axis_size("grp")
    inner = lax.axis_size("ctx")
    count = outer * inner
    poles = pole_table.shape[0]
    own = mode_index.shape[0]
    nchunk = tok // CHUNK
    groups, packed = count // GROUP, chans // GROUP // 2
    sem = pltpu.SemaphoreType.DMA
    return pl.pallas_call(
        functools.partial(kernel, outer, inner),
        out_shape=jax.ShapeDtypeStruct((tok, chans), BF16),
        in_specs=[pl.BlockSpec(memory_space=pltpu.HBM)] * 6,
        out_specs=pl.BlockSpec(memory_space=pltpu.HBM),
        scratch_shapes=[
            pltpu.VMEM((tok, chans), BF16),
            sem((tok // 128,)),
            pltpu.VMEM((tok, width3), BF16),
            pltpu.VMEM(taps.shape, F32),
            pltpu.VMEM((1, poles), F32),
            pltpu.VMEM(mode_index.shape, jnp.int32),
            pltpu.VMEM(residues.shape, F32),
            pltpu.VMEM((1, own), F32),
            sem((6,)),
            pltpu.VMEM((16, width3), BF16),
            pltpu.VMEM((groups, GROUP, own, 2 * poles), F32),
            pltpu.VMEM((own, 2 * poles), F32),
            pltpu.VMEM((GROUP, packed, 2 * poles), F32),
            pltpu.VMEM((GROUP, packed, 2 * poles), F32),
            pltpu.VMEM((groups, packed, 2 * poles), F32),
            pltpu.VMEM((GROUP, packed, 2 * poles), F32),
            pltpu.VMEM((GROUP, packed, 2 * poles), F32),
            pltpu.VMEM((tok + 8, width3), F32),
            pltpu.VMEM((chans // 128, tok, 128), F32),
            pltpu.VMEM((tok, chans), BF16),
            pltpu.VMEM((2 * CHUNK, nchunk, chans), F32),
            pltpu.VMEM((chans // 128, tok, 128), F32),
            pltpu.VMEM((tok, chans), F32),
            pltpu.VMEM((CHUNK, chans), F32),
            pltpu.VMEM((2 * poles, tok), BF16),
            pltpu.VMEM((tok, 4 * poles), BF16),
            pltpu.VMEM((CHUNK, 4 * poles), BF16),
            pltpu.VMEM((2 * poles, CHUNK), BF16),
        ] + [sem] * 12,
        compiler_params=pltpu.CompilerParams(
            collective_id=0, has_side_effects=True, vmem_limit_bytes=64 * 1024 * 1024
        ),
    )(
        seq_feats, taps, pole_table.reshape(1, poles), mode_index, residues, skip.reshape(1, own)
    )


def solution(mesh):
    return jax.shard_map(
        body,
        mesh=mesh,
        in_specs=(
            P(("grp", "ctx"), None),
            P(),
            P(),
            P(("grp", "ctx"), None),
            P(("grp", "ctx"), None),
            P(("grp", "ctx")),
        ),
        out_specs=P(("grp", "ctx"), None),
        check_vma=False,
    )
```
